512 devices in a mesh: dp: 64 (over z, y), tensor: 8 (over x, core).
Axes of the slice: x: 4, y: 4, z: 16, core: 2. Of those that a mesh axis runs over, the one named last changes fastest.
Arguments:
- queries: bfloat16 [32768, 8192], P('dp', 'tensor'), may hold values from -8 to 8
- key_heads: bfloat16 [32768, 1024], P('dp', 'tensor'), may hold values from -8 to 8
- value_heads: bfloat16 [32768, 1024], P('dp', 'tensor'), may hold values from -200 to 200
- doc_lengths: int32 [256], replicated, may hold values from 1 to 512, 32768 in all
Outputs:
- hessian: float32 [8, 1024, 1024], P('tensor', 'dp')
The draws below stay inside these ranges and needn't reach their ends.
Inputs may be any that keep to these rules, and one draw needn't show every extreme that they name: `doc_lengths`: every document fits in 512 tokens; one document has exactly 512.
All inputs are finite; a program needn't handle non-finite values.
Results may differ from the reference program's by a relative error of at most 0.0006.
Values may be sent and summed in bfloat16 or wider, within the bound.
A program may use at most 128 MiB of HBM per device.

```python
import math
import jax
import jax.numpy as jnp
import numpy as np
from jax import lax

HEADS = 64
KVH = 8
HD = 128
TOK_DEV = 512
GW = 1024
TOKENS = 32768
DOCS = 256
N_DP = 64


def draw_queries(key, part):
    key = jax.random.fold_in(key, 11)
    normal_part = jnp.clip(jax.random.normal(key, (TOKENS, HEADS * HD), jnp.float32), -6.0, 6.0)
    return normal_part.astype(jnp.bfloat16)


def draw_key_heads(key, part):
    key = jax.random.fold_in(key, 13)
    normal_part = jnp.clip(jax.random.normal(key, (TOKENS, KVH * HD), jnp.float32), -6.0, 6.0)
    return normal_part.astype(jnp.bfloat16)


def draw_value_heads(key, part):
    key = jax.random.fold_in(key, 17)
    key_base, key_rows, key_cols = jax.random.split(key, 3)
    row_trend = 3.0 ** (jnp.arange(TOKENS, dtype=jnp.float32) / TOKENS)
    row_scale = jnp.exp(jax.random.uniform(key_rows, (TOKENS,), jnp.float32, 0.0, 2.302585)) * row_trend
    col_scale = jnp.exp(jax.random.uniform(key_cols, (KVH * HD,), jnp.float32, 0.0, 2.302585))
    normal_part = jnp.clip(jax.random.normal(key_base, (TOKENS, KVH * HD), jnp.float32), -6.0, 6.0)
    return (normal_part * row_scale[:, None] * col_scale[None, :] * 0.1).astype(jnp.bfloat16)


def length_profile(count, total, reach, skew):
    loads = [(1 << 20) // math.isqrt(rank ** skew) + 1 for rank in range(2, count + 1)]
    surplus, holding = total - reach - (count - 1), [1] * (count - 1)
    while surplus > 0:
        candidates = [i for i in range(count - 1) if holding[i] < reach]
        pool, remaining = sum([loads[i] for i in candidates]), surplus
        for i in candidates:
            addition = min(reach - holding[i], max(1, remaining * loads[i] // pool), surplus)
            holding[i] = holding[i] + addition
            surplus = surplus - addition
    return np.array([reach] + holding)


def ragged(rng, count, total, most, slope):
    if count == 2:
        one = jax.random.randint(rng, (), max(1, total - most), min(most, total - 1) + 1)
        return jnp.stack([one, total - one])
    lengths = jnp.asarray(length_profile(count, total, most, slope), jnp.int32)
    couples = (count - 1) // 2
    source_of, taker = lengths[1:1 + 2 * couples:2], lengths[2:2 + 2 * couples:2]
    margin = jnp.minimum(source_of - 1, most - taker)
    moved = jax.random.randint(jax.random.fold_in(rng, 1), (couples,), 0, 1 << 20) % (margin + 1)
    lengths = lengths.at[1:1 + 2 * couples:2].set(source_of - moved).at[2:2 + 2 * couples:2].set(taker + moved)
    return lengths[jax.random.permutation(jax.random.fold_in(rng, 2), count)]


def setup_inputs(seed: int = 0) -> dict:
    key_of = jax.random.split(jax.random.key(seed), 5)
    queries = draw_queries(jax.random.fold_in(key_of[4], 71), 0)
    key_heads = draw_key_heads(jax.random.fold_in(key_of[4], 71), 0)
    value_heads = draw_value_heads(jax.random.fold_in(key_of[4], 71), 0)
    doc_lengths = ragged(key_of[3], DOCS, TOKENS, TOK_DEV, 2).astype(jnp.int32)
    return dict(queries=queries, key_heads=key_heads, value_heads=value_heads, doc_lengths=doc_lengths)


damping = 0.01

def doc_start_of(positions, starts):
    return lax.optimization_barrier(jnp.max(jnp.where(starts[None, :] <= positions[:, None], starts[None, :], 0), axis=1))

def attend_block(queries, key_pad, value_pad, starts, block):
    inv_root = 1.0 / math.sqrt(HD)
    first_row = block * TOK_DEV
    query_rows = lax.dynamic_slice_in_dim(queries, first_row, TOK_DEV, 0).astype(jnp.float32)
    query_rows = query_rows.reshape(TOK_DEV, KVH, HEADS // KVH, HD)
    key_rows = lax.dynamic_slice_in_dim(key_pad, first_row, 2 * TOK_DEV, 0).astype(jnp.float32)
    key_rows = key_rows.reshape(2 * TOK_DEV, KVH, HD)
    value_rows = lax.dynamic_slice_in_dim(value_pad, first_row, 2 * TOK_DEV, 0).astype(jnp.float32)
    value_rows = value_rows.reshape(2 * TOK_DEV, KVH, HD)
    query_pos = first_row + jnp.arange(TOK_DEV, dtype=jnp.int32)
    key_pos = first_row - TOK_DEV + jnp.arange(2 * TOK_DEV, dtype=jnp.int32)
    doc_start = doc_start_of(query_pos, starts)
    visible = (key_pos[None, :] >= doc_start[:, None]) & (key_pos[None, :] <= query_pos[:, None])
    scores = jnp.einsum('tgqd,sgd->gqts', query_rows, key_rows) * inv_root
    scores = jnp.where(visible[None, None], scores, -1e+30)
    row_peak = lax.optimization_barrier(jnp.max(scores, axis=-1))
    exponent = jnp.exp(scores - row_peak[..., None])
    row_total = lax.optimization_barrier(jnp.sum(exponent, axis=-1))
    weights = exponent.astype(jnp.bfloat16)
    weights = lax.optimization_barrier(weights).astype(jnp.float32)
    blended = jnp.einsum('gqts,sgd->tgqd', weights, value_rows)
    blended = blended / jnp.transpose(row_total, (2, 0, 1))[..., None]
    return blended.astype(jnp.bfloat16).reshape(TOK_DEV, HEADS * HD)

def reference(queries, key_heads, value_heads, doc_lengths):
    starts = jnp.cumsum(doc_lengths, dtype=jnp.int32) - doc_lengths
    zero_rows = jnp.zeros((TOK_DEV, KVH * HD), jnp.bfloat16)
    key_pad = jnp.concatenate([zero_rows, key_heads], axis=0)
    value_pad = jnp.concatenate([zero_rows, value_heads], axis=0)
    attended = lax.map(lambda block: attend_block(queries, key_pad, value_pad, starts, block), jnp.arange(N_DP, dtype=jnp.int32))
    attended = attended.reshape(TOKENS, KVH, GW)
    energy = jnp.sum(jnp.square(attended.astype(jnp.float32)))
    grouped = jnp.transpose(attended, (1, 0, 2))
    gram = lax.map(lambda group: jnp.dot(group.T, group, preferred_element_type=jnp.float32), grouped)
    eye_block = jnp.eye(GW, dtype=jnp.float32)
    return gram * (HEADS * HD / energy) + damping * eye_block[None]
```

```python
import functools
import math

import jax
import jax.numpy as jnp
from jax import lax
from jax.experimental import pallas as pl
from jax.experimental.pallas import tpu as pltpu
from jax.sharding import PartitionSpec as P

HEADS = 64
HD = 128
TOK = 512
QB = 128
WIN = TOK + QB
NZ, NY, NT = 16, 4, 8
PAIRS = 4
FULL = 32767.0
MESH = pl.DeviceIdType.MESH
F32 = jnp.float32

damping = 0.01


def passed_along(value, axis, steps):
    count = lax.axis_size(axis)
    first, last = (max(0, -steps), min(count, count - steps))
    return lax.ppermute(value, axis, [(source, source + steps) for source in range(first, last)])


def z_of(pair, quarter):
    return 2 * pair + quarter % 2 + 8 * (quarter // 2)


def piece_blocks(stage, part):
    if part == 0:
        return stage * stage, [(stage, col) for col in range(stage + 1)]
    return stage * stage + stage + 1, [(row, stage) for row in range(stage)]


PIECES = [(s, p) for s in range(PAIRS) for p in range(2) if p == 0 or s > 0]


def to_fixed(block):
    peak = jnp.maximum(jnp.max(jnp.abs(block), axis=0, keepdims=True), 1e-30)
    fixed = jnp.round(block * (FULL / peak)).astype(jnp.int32).astype(jnp.int16)
    return fixed, peak * (1.0 / FULL)


def from_fixed(fixed, scale):
    return fixed.astype(jnp.int32).astype(F32) * scale


def kernel(
    len_ref, q_ref, kp_ref, ko_ref, vp_ref, vo_ref, out_ref,
    keys, vt, bias, at, gs, own, yq, yqs, yr, yrs, zq, zqs, zr, zrs, en, ent, eny, enz,
    y_send, y_recv, z_send, z_recv, e_send, e_recv,
):
    dp = lax.axis_index("dp")
    t = lax.axis_index("tensor")
    z, y = lax.div(dp, NY), lax.rem(dp, NY)
    first_row = dp * TOK

    def z_peer(d):
        return (lax.rem(z + d, NZ) * NY + y, t)

    def y_peer(d):
        return (z * NY + lax.rem(y + d, NY), t)

    def t_peer(d):
        return (dp, lax.rem(t + d, NT))

    barrier = pltpu.get_barrier_semaphore()
    peers = [y_peer(d) for d in range(1, NY)] + [t_peer(d) for d in range(1, NT)]
    peers += [z_peer(d) for d in range(1, NZ)]
    for peer in peers:
        pl.semaphore_signal(barrier, inc=1, device_id=peer, device_id_type=MESH)

    def remote(src, dst, send, recv, peer):
        return pltpu.make_async_remote_copy(
            src_ref=src, dst_ref=dst, send_sem=send, recv_sem=recv, device_id=peer, device_id_type=MESH
        )

    def wait_for(ref, sem):
        pltpu.make_async_copy(ref, ref, sem).wait()

    keys[0:TOK] = kp_ref[...]
    keys[TOK:] = ko_ref[...]
    vt[:, 0:TOK] = vp_ref[...].T
    vt[:, TOK:] = vo_ref[...].T

    lens = len_ref[...].astype(F32)
    n_docs = lens.shape[1]
    before = lax.broadcasted_iota(jnp.int32, (n_docs, n_docs), 1) < lax.broadcasted_iota(
        jnp.int32, (n_docs, n_docs), 0
    )
    starts = jnp.sum(jnp.where(before, lens, 0.0), axis=1, keepdims=True)
    position = (first_row + lax.broadcasted_iota(jnp.int32, (1, TOK), 1)).astype(F32)
    doc_start = jnp.max(jnp.where(starts <= position, starts, 0.0), axis=0, keepdims=True)
    for b in range(TOK // QB):
        key_pos = (first_row - TOK + b * QB + lax.broadcasted_iota(jnp.int32, (WIN, QB), 0)).astype(F32)
        cols = slice(b * QB, (b + 1) * QB)
        visible = (key_pos >= doc_start[:, cols]) & (key_pos <= position[:, cols])
        bias[b] = jnp.where(visible, 0.0, -1e30)

    factor = math.log2(math.e) / math.sqrt(HD)

    def attend(pair, b, energy):
        rows = pl.ds(pl.multiple_of(b * QB, QB), QB)
        window = pl.ds(pl.multiple_of(b * QB, QB), WIN)
        two = jnp.concatenate(
            [q_ref[rows, h * HD : (h + 1) * HD] for h in (pair, pair + PAIRS)], axis=0
        )
        scores = lax.dot_general(
            keys[window, :], two, (((1,), (1,)), ((), ())), preferred_element_type=F32
        )
        mask = bias[b]
        scores = scores * factor + jnp.concatenate([mask, mask], axis=1)
        peak = jnp.max(scores, axis=0, keepdims=True)
        exponent = jnp.exp2(scores - peak)
        total = jnp.sum(exponent, axis=0, keepdims=True)
        blended = lax.dot_general(
            vt[:, window], exponent.astype(jnp.bfloat16), (((1,), (0,)), ((), ())), preferred_element_type=F32
        )
        attended = (blended * (1.0 / total)).astype(jnp.bfloat16)
        at[pair, 0:HD, rows] = attended[:, 0:QB]
        at[pair, HD:, rows] = attended[:, QB:]
        wide = attended.astype(F32)
        return energy + jnp.sum(wide * wide, axis=0, keepdims=True)

    def gram_block(k, row, col):
        block = lax.dot_general(at[row], at[col], (((1,), (1,)), ((), ())), preferred_element_type=F32)
        gs[...] = block
        fixed, scale = to_fixed(block)
        yqs[k] = scale
        for q in range(4):
            for a in range(NY):
                low = q * 64 + a * 16
                yq[a, k, q * 16 : (q + 1) * 16, :] = fixed[low : low + 16, :]
            own[k, q * 16 : (q + 1) * 16, :] = gs[pl.ds(pl.multiple_of(q * 64 + y * 16, 16), 16), :]

    def y_stage(piece):
        first, blocks = piece_blocks(*PIECES[piece])
        for i, (row, col) in enumerate(blocks):
            gram_block(first + i, row, col)
        span = pl.ds(first, len(blocks))
        for d in range(1, NY):
            peer = y_peer(d)
            to = lax.rem(y + d, NY)
            remote(yqs.at[span], yrs.at[d - 1, span], y_send.at[1, piece], y_recv.at[1, piece], peer).start()
            remote(yq.at[to, span], yr.at[d - 1, span], y_send.at[0, piece], y_recv.at[0, piece], peer).start()

    sent = []

    def z_stage(piece):
        stage, part = PIECES[piece]
        first, blocks = piece_blocks(stage, part)
        span = pl.ds(first, len(blocks))
        wait_for(yrs.at[:, span], y_recv.at[1, piece])
        wait_for(yr.at[:, span], y_recv.at[0, piece])
        for k in range(first, first + len(blocks)):
            total = own[k]
            for d in range(NY - 1):
                total = total + from_fixed(yr[d, k], yrs[d, k])
            own[k] = total
            fixed, scale = to_fixed(total)
            zqs[k] = scale
            for q in range(4):
                zq[k, q] = fixed[q * 16 : (q + 1) * 16, :]
        if part == 0:
            targets = [(stage, first, len(blocks), 0)]
        else:
            targets = [(row, first + row, 1, stage) for row in range(stage)]
        for row, k, count, slot in targets:
            for q in range(4):
                target = z_of(row, q)
                n = len(sent)
                place = lax.rem(z - target + NZ, NZ) - 1

                def copies(target=target, n=n, place=place, q=q, k=k, count=count, slot=slot):
                    kinds = (
                        (zq.at[pl.ds(k, count), q], zr.at[place, pl.ds(slot, count)]),
                        (zqs.at[pl.ds(k, count)], zrs.at[place, pl.ds(slot, count)]),
                    )
                    sem = slot if part == 1 else 0
                    return [
                        remote(src, dst, z_send.at[i, n], z_recv.at[i, sem], (target * NY + y, t))
                        for i, (src, dst) in enumerate(kinds)
                    ]

                sent.append((target, copies))

                @pl.when(z != target)
                def _(copies=copies):
                    for copy in copies():
                        copy.start()

    energy = jnp.zeros((1, 2 * QB), F32)
    for pair in range(PAIRS):
        energy = lax.fori_loop(0, TOK // QB, functools.partial(attend, pair), energy)
        if pair == 0:
            pl.semaphore_wait(barrier, len(peers))
        if pair == PAIRS - 1:
            en[0] = energy[:, 0:QB] + energy[:, QB:]
            for d in range(1, NT):
                remote(en.at[0], ent.at[d - 1], e_send.at[0], e_recv.at[0], t_peer(d)).start()
        for piece, (stage, part) in enumerate(PIECES):
            if stage == pair - 2:
                z_stage(piece)
        for piece, (stage, part) in enumerate(PIECES):
            if stage == pair:
                y_stage(piece)
    wait_for(ent, e_recv.at[0])
    en[1] = en[0] + jnp.sum(ent[...], axis=0)
    for d in range(1, NY):
        remote(en.at[1], eny.at[d - 1], e_send.at[1], e_recv.at[1], y_peer(d)).start()
    for piece, (stage, part) in enumerate(PIECES):
        if stage == PAIRS - 2:
            z_stage(piece)
    wait_for(eny, e_recv.at[1])
    en[2] = en[1] + jnp.sum(eny[...], axis=0)
    for d in range(1, NZ):
        remote(en.at[2], enz.at[d - 1], e_send.at[2], e_recv.at[2], z_peer(d)).start()
    for piece, (stage, part) in enumerate(PIECES):
        if stage == PAIRS - 1:
            z_stage(piece)

    my_pair = lax.div(lax.rem(z, 8), 2)
    my_quarter = 2 * lax.div(z, 8) + lax.rem(z, 2)
    wait_for(enz, e_recv.at[2])
    all_energy = jnp.sum(en[2] + jnp.sum(enz[...], axis=0), axis=1, keepdims=True)
    gain = (HEADS * HD) / all_energy
    for s in range(PAIRS):

        @pl.when(my_pair == s)
        def _(s=s):
            wait_for(zrs.at[:, pl.ds(0, s + 1)], z_recv.at[1, 0])
            wait_for(zr.at[:, pl.ds(0, s + 1)], z_recv.at[0, 0])

    for s in range(1, PAIRS):

        @pl.when(my_pair < s)
        def _(s=s):
            wait_for(zrs.at[:, s], z_recv.at[1, s])
            wait_for(zr.at[:, s], z_recv.at[0, s])

    row_id = dp * 16 + lax.broadcasted_iota(jnp.int32, (16, HD), 0)
    col_id = lax.broadcasted_iota(jnp.int32, (16, HD), 1)
    my_rows = pl.ds(pl.multiple_of(my_quarter * 16, 16), 16)
    for col in range(PAIRS):
        k = jnp.where(my_pair >= col, my_pair * my_pair + col, col * col + col + 1 + my_pair)
        total = own[k, my_rows, :]
        for d in range(NZ - 1):
            total = total + from_fixed(zr[d, col], zrs[d, col])
        for half in range(2):
            head = col + PAIRS * half
            part = total[:, half * HD : (half + 1) * HD] * gain
            eye = jnp.where(row_id == col_id + head * HD, damping, 0.0)
            out_ref[:, head * HD : (head + 1) * HD] = part + eye

    for piece, (stage, part) in enumerate(PIECES):
        first, blocks = piece_blocks(stage, part)
        span = pl.ds(first, len(blocks))
        wait_for(yrs.at[:, span], y_send.at[1, piece])
        wait_for(yr.at[:, span], y_send.at[0, piece])
    for target, copies in sent:

        @pl.when(z != target)
        def _(copies=copies):
            for copy in copies():
                copy.wait_send()

    wait_for(ent, e_send.at[0])
    wait_for(eny, e_send.at[1])
    wait_for(enz, e_send.at[2])


def on_device(queries, key_heads, value_heads, doc_lengths):
    prev_keys, prev_values = passed_along((key_heads, value_heads), "dp", 1)
    blocks = PAIRS * PAIRS
    width = 2 * HD
    n_sent = sum(len(piece_blocks(s, 1)[1]) + 1 for s in range(PAIRS)) * 4
    vmem = pl.BlockSpec(memory_space=pltpu.VMEM)
    rows = pl.pallas_call(
        kernel,
        out_shape=jax.ShapeDtypeStruct((16, 8 * HD), F32),
        in_specs=[vmem] * 6,
        out_specs=vmem,
        scratch_shapes=[
            pltpu.VMEM((2 * TOK, HD), jnp.bfloat16),
            pltpu.VMEM((HD, 2 * TOK), jnp.bfloat16),
            pltpu.VMEM((TOK // QB, WIN, QB), F32),
            pltpu.VMEM((PAIRS, width, TOK), jnp.bfloat16),
            pltpu.VMEM((width, width), F32),
            pltpu.VMEM((blocks, 64, width), F32),
            pltpu.VMEM((NY, blocks, 64, width), jnp.int16),
            pltpu.VMEM((blocks, 1, width), F32),
            pltpu.VMEM((NY - 1, blocks, 64, width), jnp.int16),
            pltpu.VMEM((NY - 1, blocks, 1, width), F32),
            pltpu.VMEM((blocks, 4, 16, width), jnp.int16),
            pltpu.VMEM((blocks, 1, width), F32),
            pltpu.VMEM((NZ - 1, PAIRS, 16, width), jnp.int16),
            pltpu.VMEM((NZ - 1, PAIRS, 1, width), F32),
            pltpu.VMEM((3, 1, HD), F32),
            pltpu.VMEM((NT - 1, 1, HD), F32),
            pltpu.VMEM((NY - 1, 1, HD), F32),
            pltpu.VMEM((NZ - 1, 1, HD), F32),
            pltpu.SemaphoreType.DMA((2, len(PIECES))),
            pltpu.SemaphoreType.DMA((2, len(PIECES))),
            pltpu.SemaphoreType.DMA((2, n_sent)),
            pltpu.SemaphoreType.DMA((2, PAIRS)),
            pltpu.SemaphoreType.DMA((3,)),
            pltpu.SemaphoreType.DMA((3,)),
        ],
        compiler_params=pltpu.CompilerParams(
            collective_id=0, has_side_effects=True, vmem_limit_bytes=48 << 20
        ),
        name="attend_and_gram",
    )(doc_lengths.reshape(1, -1), queries, prev_keys, key_heads, prev_values, value_heads)
    return rows[None]


def solution(mesh):
    placed = (P("dp", "tensor"), P("dp", "tensor"), P("dp", "tensor"), P())
    return jax.shard_map(
        on_device, mesh=mesh, in_specs=placed, out_specs=P("tensor", "dp", None), check_vma=False
    )
```

```python
import functools
import math

import jax
import jax.numpy as jnp
from jax import lax
from jax.experimental import pallas as pl
from jax.experimental.pallas import tpu as pltpu
from jax.sharding import PartitionSpec as P

HEADS = 64
HD = 128
TOK = 512
QB = 128
WIN = TOK + QB
NZ, NY, NT = 16, 4, 8
PAIRS = 4
FULL = 32767.0
MESH = pl.DeviceIdType.MESH
F32 = jnp.float32

damping = 0.01


RELAYS = (1, 5, 15, 11)
INPUTS = ((2, 3, 4), (6, 7, 8), (14, 13, 12), (10, 9))


def plan():
    pieces = []
    for stage in range(PAIRS):
        row = [(stage, col) for col in range(stage + 1)]
        if stage == PAIRS - 1:
            pieces.append((stage, row))
        else:
            pieces.append((stage, row))
        if stage > 0:
            pieces.append((stage, [(above, stage) for above in range(stage)]))
    return pieces


PIECES = plan()
FIRST = [sum(len(blocks) for _, blocks in PIECES[:n]) for n in range(len(PIECES))]
NUMBER = {block: k for k, block in enumerate(block for _, blocks in PIECES for block in blocks)}


def to_fixed(block):
    peak = jnp.maximum(jnp.max(jnp.abs(block), axis=0, keepdims=True), 1e-30)
    fixed = jnp.round(block * (FULL / peak)).astype(jnp.int32).astype(jnp.int16)
    return fixed, peak * (1.0 / FULL)


def from_fixed(fixed, scale):
    return fixed.astype(jnp.int32).astype(F32) * scale


def kernel(
    len_hbm, q_hbm, k_hbm, v_hbm, out_ref,
    lengths, q_ref, keys, vals, vt, bias, at, gs, own,
    yq, yqs, yr, yrs, zq, zqs, rr, rrs, rq, rqs, zr, zrs, en, ent, eny, enz,
    l_sem, h_send, h_recv, y_send, y_recv, r_send, r_recv, z_send, z_recv, e_send, e_recv,
):
    dp = lax.axis_index("dp")
    t = lax.axis_index("tensor")
    z, y = lax.div(dp, NY), lax.rem(dp, NY)
    first_row = dp * TOK

    def z_peer(d):
        return (lax.rem(z + d, NZ) * NY + y, t)

    def y_peer(d):
        return (z * NY + lax.rem(y + d, NY), t)

    def t_peer(d):
        return (dp, lax.rem(t + d, NT))

    following = (lax.rem(dp + 1, NZ * NY), t)
    preceding = (lax.rem(dp + NZ * NY - 1, NZ * NY), t)
    barrier = pltpu.get_barrier_semaphore()
    peers = [preceding] + [y_peer(d) for d in range(1, NY)] + [z_peer(d) for d in range(1, NZ)]
    peers += [t_peer(d) for d in range(1, NT)]
    for peer in peers:
        pl.semaphore_signal(barrier, inc=1, device_id=peer, device_id_type=MESH)

    def remote(src, dst, send, recv, peer):
        return pltpu.make_async_remote_copy(
            src_ref=src, dst_ref=dst, send_sem=send, recv_sem=recv, device_id=peer, device_id_type=MESH
        )

    def wait_for(ref, sem):
        pltpu.make_async_copy(ref, ref, sem).wait()

    earlier, later = pl.ds(0, TOK), pl.ds(TOK, TOK)
    loads = [(len_hbm, lengths), (k_hbm, keys.at[later]), (v_hbm, vals.at[later]), (q_hbm, q_ref)]
    loads = [pltpu.make_async_copy(src, dst, l_sem.at[n]) for n, (src, dst) in enumerate(loads)]
    for load in loads:
        load.start()

    pl.semaphore_wait(barrier, len(peers))
    halo = [
        remote(k_hbm, keys.at[earlier], h_send.at[0], h_recv.at[0], following),
        remote(v_hbm, vals.at[earlier], h_send.at[1], h_recv.at[1], following),
    ]
    for copy in halo:
        copy.start()

    loads[0].wait()
    lens = lengths[...].astype(F32)
    n_docs = lens.shape[1]
    before = lax.broadcasted_iota(jnp.int32, (n_docs, n_docs), 1) < lax.broadcasted_iota(
        jnp.int32, (n_docs, n_docs), 0
    )
    starts = jnp.sum(jnp.where(before, lens, 0.0), axis=1, keepdims=True)
    position = (first_row + lax.broadcasted_iota(jnp.int32, (1, TOK), 1)).astype(F32)
    doc_start = jnp.max(jnp.where(starts <= position, starts, 0.0), axis=0, keepdims=True)
    for b in range(TOK // QB):
        key_pos = (first_row - TOK + b * QB + lax.broadcasted_iota(jnp.int32, (WIN, QB), 0)).astype(F32)
        cols = slice(b * QB, (b + 1) * QB)
        visible = (key_pos >= doc_start[:, cols]) & (key_pos <= position[:, cols])
        bias[b] = jnp.where(visible, 0.0, -1e30)
    for load in loads[1:]:
        load.wait()
    vt[:, TOK:] = vals[TOK:].T
    for copy in halo:
        copy.wait_recv()
    vt[:, 0:TOK] = vals[0:TOK].T

    factor = math.log2(math.e) / math.sqrt(HD)

    def attend(pair, b, energy):
        rows = pl.ds(pl.multiple_of(b * QB, QB), QB)
        window = pl.ds(pl.multiple_of(b * QB, QB), WIN)
        two = jnp.concatenate(
            [q_ref[rows, h * HD : (h + 1) * HD] for h in (pair, pair + PAIRS)], axis=0
        )
        scores = lax.dot_general(
            keys[window, :], two, (((1,), (1,)), ((), ())), preferred_element_type=F32
        )
        mask = bias[b]
        scores = scores * factor + jnp.concatenate([mask, mask], axis=1)
        peak = jnp.max(scores, axis=0, keepdims=True)
        exponent = jnp.exp2(scores - peak)
        total = jnp.sum(exponent, axis=0, keepdims=True)
        blended = lax.dot_general(
            vt[:, window], exponent.astype(jnp.bfloat16), (((1,), (0,)), ((), ())), preferred_element_type=F32
        )
        attended = (blended * (1.0 / total)).astype(jnp.bfloat16)
        at[pair, 0:HD, rows] = attended[:, 0:QB]
        at[pair, HD:, rows] = attended[:, QB:]
        wide = attended.astype(F32)
        return energy + jnp.sum(wide * wide, axis=0, keepdims=True)

    def gram_block(k, row, col):
        block = lax.dot_general(at[row], at[col], (((1,), (1,)), ((), ())), preferred_element_type=F32)
        gs[...] = block
        fixed, scale = to_fixed(block)
        yqs[k] = scale
        for q in range(4):
            for a in range(NY):
                low = q * 64 + a * 16
                yq[a, k, q * 16 : (q + 1) * 16, :] = fixed[low : low + 16, :]
            own[k, q * 16 : (q + 1) * 16, :] = gs[pl.ds(pl.multiple_of(q * 64 + y * 16, 16), 16), :]

    def y_stage(piece):
        first, blocks = FIRST[piece], PIECES[piece][1]
        for i, (row, col) in enumerate(blocks):
            gram_block(first + i, row, col)
        span = pl.ds(first, len(blocks))
        for d in range(1, NY):
            peer = y_peer(d)
            to = lax.rem(y + d, NY)
            remote(yqs.at[span], yrs.at[d - 1, span], y_send.at[1, piece], y_recv.at[1, piece], peer).start()
            remote(yq.at[to, span], yr.at[d - 1, span], y_send.at[0, piece], y_recv.at[0, piece], peer).start()

    def z_stage(piece):
        first, blocks = FIRST[piece], PIECES[piece][1]
        span = pl.ds(first, len(blocks))
        wait_for(yrs.at[:, span], y_recv.at[1, piece])
        wait_for(yr.at[:, span], y_recv.at[0, piece])
        for k in range(first, first + len(blocks)):
            total = own[k]
            for d in range(NY - 1):
                total = total + from_fixed(yr[d, k], yrs[d, k])
            own[k] = total
            fixed, scale = to_fixed(total)
            zqs[k] = scale
            for q in range(4):
                zq[k, q] = fixed[q * 16 : (q + 1) * 16, :]
        for role, offsets in enumerate(INPUTS):
            for n, offset in enumerate(offsets):

                def forward(blocks, quarter, slots, role=role, n=n, offset=offset):
                    peer = z_peer(NZ - offset + RELAYS[role])
                    i = 3 * role + n
                    col = slots.start
                    remote(
                        zqs.at[blocks], rrs.at[role, n, slots], r_send.at[1, i], r_recv.at[1, role, col], peer
                    ).start()
                    remote(
                        zq.at[blocks, quarter], rr.at[role, n, slots], r_send.at[0, i], r_recv.at[0, role, col], peer
                    ).start()

                for_owner(piece, offset, forward)

    def for_owner(piece, offset, action):
        stage, blocks = PIECES[piece]
        owner = lax.rem(z + NZ - offset, NZ)
        pair = lax.div(lax.rem(owner, 8), 2)
        quarter = 2 * lax.div(owner, 8) + lax.rem(owner, 2)
        if blocks[0][0] == stage:

            @pl.when(pair == stage)
            def _():
                action(pl.ds(FIRST[piece], len(blocks)), quarter, pl.ds(blocks[0][1], len(blocks)))

        else:

            @pl.when(pair < stage)
            def _():
                action(pl.ds(FIRST[piece] + pair, 1), quarter, pl.ds(stage, 1))

    def z_relay(piece):
        for role, offset in enumerate(RELAYS):

            def pass_on(blocks, quarter, slots, role=role, offset=offset):
                inputs, col = len(INPUTS[role]), slots.start
                wait_for(rrs.at[role, pl.ds(0, inputs), slots], r_recv.at[1, role, col])
                wait_for(rr.at[role, pl.ds(0, inputs), slots], r_recv.at[0, role, col])
                rows = pl.ds(pl.multiple_of(quarter * 16, 16), 16)
                for i in range(slots.size):
                    total = own[blocks.start + i, rows, :]
                    for n in range(inputs):
                        total = total + from_fixed(rr[role, n, col + i], rrs[role, n, col + i])
                    rq[role, col + i], rqs[role, col + i] = to_fixed(total)
                peer = z_peer(NZ - offset)
                remote(rqs.at[role, slots], zrs.at[role, slots], z_send.at[1, role], z_recv.at[1, col], peer).start()
                remote(rq.at[role, slots], zr.at[role, slots], z_send.at[0, role], z_recv.at[0, col], peer).start()

            for_owner(piece, offset, pass_on)

    def of_stage(stage, step):
        for piece, (its_stage, _) in enumerate(PIECES):
            if its_stage == stage:
                step(piece)

    def spread(n, landing, peer):
        for d in range(1, landing.shape[0] + 1):
            remote(en.at[n], landing.at[d - 1], e_send.at[n], e_recv.at[n], peer(d)).start()

    def gather(n, landing):
        wait_for(landing, e_recv.at[n])
        return en[n] + jnp.sum(landing[...], axis=0)

    energy = jnp.zeros((1, 2 * QB), F32)
    for pair in range(PAIRS):
        energy = lax.fori_loop(0, TOK // QB, functools.partial(attend, pair), energy, unroll=4)
        if pair == PAIRS - 1:
            en[0] = energy[:, 0:QB] + energy[:, QB:]
            spread(0, enz, z_peer)
        of_stage(pair - 3, z_relay)
        of_stage(pair - 2, z_stage)
        of_stage(pair, y_stage)
    last = [piece for piece, (stage, _) in enumerate(PIECES) if stage == PAIRS - 1]
    of_stage(PAIRS - 3, z_relay)
    of_stage(PAIRS - 2, z_stage)
    en[1] = gather(0, enz)
    spread(1, ent, t_peer)
    of_stage(PAIRS - 2, z_relay)
    z_stage(last[0])
    en[2] = gather(1, ent)
    spread(2, eny, y_peer)
    z_stage(last[1])
    z_relay(last[0])
    z_relay(last[1])

    my_pair = lax.div(lax.rem(z, 8), 2)
    my_quarter = 2 * lax.div(z, 8) + lax.rem(z, 2)
    all_energy = jnp.sum(gather(2, eny), axis=1, keepdims=True)
    gain = (HEADS * HD) / all_energy
    for piece in range(len(PIECES)):

        def arrive(blocks, quarter, slots):
            wait_for(zrs.at[:, slots], z_recv.at[1, slots.start])
            wait_for(zr.at[:, slots], z_recv.at[0, slots.start])

        for_owner(piece, 0, arrive)

    row_id = dp * 16 + lax.broadcasted_iota(jnp.int32, (16, HD), 0)
    col_id = lax.broadcasted_iota(jnp.int32, (16, HD), 1)
    my_rows = pl.ds(pl.multiple_of(my_quarter * 16, 16), 16)
    for col in range(PAIRS):
        k = sum(jnp.where(my_pair == row, NUMBER[row, col], 0) for row in range(PAIRS))
        total = own[k, my_rows, :]
        for role in range(len(RELAYS)):
            total = total + from_fixed(zr[role, col], zrs[role, col])
        for half in range(2):
            head = col + PAIRS * half
            part = total[:, half * HD : (half + 1) * HD] * gain
            eye = jnp.where(row_id == col_id + head * HD, damping, 0.0)
            out_ref[:, head * HD : (head + 1) * HD] = part + eye

    for copy in halo:
        copy.wait_send()
    for piece, (_, blocks) in enumerate(PIECES):
        span = pl.ds(FIRST[piece], len(blocks))
        wait_for(yrs.at[:, span], y_send.at[1, piece])
        wait_for(yr.at[:, span], y_send.at[0, piece])
    for role, offsets in enumerate(INPUTS):
        for n in range(len(offsets)):
            wait_for(rrs.at[role, n], r_send.at[1, 3 * role + n])
            wait_for(rr.at[role, n], r_send.at[0, 3 * role + n])
        wait_for(zrs.at[role], z_send.at[1, role])
        wait_for(zr.at[role], z_send.at[0, role])
    for n, landing in enumerate((enz, ent, eny)):
        wait_for(landing, e_send.at[n])


def on_device(queries, key_heads, value_heads, doc_lengths):
    blocks = PAIRS * PAIRS
    width = 2 * HD
    roles = len(RELAYS)
    vmem = pl.BlockSpec(memory_space=pltpu.VMEM)
    rows = pl.pallas_call(
        kernel,
        out_shape=jax.ShapeDtypeStruct((16, 8 * HD), F32),
        in_specs=[pl.BlockSpec(memory_space=pl.ANY)] * 4,
        out_specs=vmem,
        scratch_shapes=[
            pltpu.VMEM((1, doc_lengths.shape[0]), jnp.int32),
            pltpu.VMEM((TOK, 8 * HD), jnp.bfloat16),
            pltpu.VMEM((2 * TOK, HD), jnp.bfloat16),
            pltpu.VMEM((2 * TOK, HD), jnp.bfloat16),
            pltpu.VMEM((HD, 2 * TOK), jnp.bfloat16),
            pltpu.VMEM((TOK // QB, WIN, QB), F32),
            pltpu.VMEM((PAIRS, width, TOK), jnp.bfloat16),
            pltpu.VMEM((width, width), F32),
            pltpu.VMEM((blocks, 64, width), F32),
            pltpu.VMEM((NY, blocks, 64, width), jnp.int16),
            pltpu.VMEM((blocks, 1, width), F32),
            pltpu.VMEM((NY - 1, blocks, 64, width), jnp.int16),
            pltpu.VMEM((NY - 1, blocks, 1, width), F32),
            pltpu.VMEM((blocks, 4, 16, width), jnp.int16),
            pltpu.VMEM((blocks, 1, width), F32),
            pltpu.VMEM((roles, 3, PAIRS, 16, width), jnp.int16),
            pltpu.VMEM((roles, 3, PAIRS, 1, width), F32),
            pltpu.VMEM((roles, PAIRS, 16, width), jnp.int16),
            pltpu.VMEM((roles, PAIRS, 1, width), F32),
            pltpu.VMEM((roles, PAIRS, 16, width), jnp.int16),
            pltpu.VMEM((roles, PAIRS, 1, width), F32),
            pltpu.VMEM((3, 1, HD), F32),
            pltpu.VMEM((NT - 1, 1, HD), F32),
            pltpu.VMEM((NY - 1, 1, HD), F32),
            pltpu.VMEM((NZ - 1, 1, HD), F32),
            pltpu.SemaphoreType.DMA((4,)),
            pltpu.SemaphoreType.DMA((2,)),
            pltpu.SemaphoreType.DMA((2,)),
            pltpu.SemaphoreType.DMA((2, len(PIECES))),
            pltpu.SemaphoreType.DMA((2, len(PIECES))),
            pltpu.SemaphoreType.DMA((2, 3 * roles)),
            pltpu.SemaphoreType.DMA((2, roles, PAIRS)),
            pltpu.SemaphoreType.DMA((2, roles)),
            pltpu.SemaphoreType.DMA((2, PAIRS)),
            pltpu.SemaphoreType.DMA((3,)),
            pltpu.SemaphoreType.DMA((3,)),
        ],
        compiler_params=pltpu.CompilerParams(
            collective_id=0, has_side_effects=True, vmem_limit_bytes=60 << 20
        ),
        name="attend_and_gram",
    )(doc_lengths.reshape(1, -1), queries, key_heads, value_heads)
    return rows[None]


def solution(mesh):
    placed = (P("dp", "tensor"), P("dp", "tensor"), P("dp", "tensor"), P())
    return jax.shard_map(
        on_device, mesh=mesh, in_specs=placed, out_specs=P("tensor", "dp", None), check_vma=False
    )
```

```python
import functools
import math

import jax
import jax.numpy as jnp
from jax import lax
from jax.experimental import pallas as pl
from jax.experimental.pallas import tpu as pltpu
from jax.sharding import PartitionSpec as P

HEADS = 64
HD = 128
TOK = 512
QB = 128
WIN = TOK + QB
NZ, NY, NT = 16, 4, 8
PAIRS = 4
FULL = 32767.0
MESH = pl.DeviceIdType.MESH
F32 = jnp.float32

damping = 0.01


RELAYS = (1, 5, 15, 11)
INPUTS = ((2, 3, 4), (6, 7, 8), (14, 13, 12), (10, 9))


def plan():
    pieces = []
    for stage in range(PAIRS):
        row = [(stage, col) for col in range(stage + 1)]
        if stage == PAIRS - 1:
            pieces.append((stage, row))
        else:
            pieces.append((stage, row))
        if stage > 0:
            pieces.append((stage, [(above, stage) for above in range(stage)]))
    return pieces


PIECES = plan()
FIRST = [sum(len(blocks) for _, blocks in PIECES[:n]) for n in range(len(PIECES))]
NUMBER = {block: k for k, block in enumerate(block for _, blocks in PIECES for block in blocks)}


def to_fixed(block):
    peak = jnp.maximum(jnp.max(jnp.abs(block), axis=0, keepdims=True), 1e-30)
    fixed = jnp.round(block * (FULL / peak)).astype(jnp.int32).astype(jnp.int16)
    return fixed, peak * (1.0 / FULL)


def from_fixed(fixed, scale):
    return fixed.astype(jnp.int32).astype(F32) * scale


def kernel(
    len_hbm, q_hbm, k_hbm, v_hbm, out_ref,
    lengths, q_ref, keys, vals, vt, bias, at, gs, own,
    yq, yqs, yr, yrs, zq, zqs, rr, rrs, rq, rqs, zr, zrs, en, ent, eny, enz,
    l_sem, h_send, h_recv, y_send, y_recv, r_send, r_recv, z_send, z_recv, e_send, e_recv,
):
    dp = lax.axis_index("dp")
    t = lax.axis_index("tensor")
    z, y = lax.div(dp, NY), lax.rem(dp, NY)
    first_row = dp * TOK

    def z_peer(d):
        return (lax.rem(z + d, NZ) * NY + y, t)

    def y_peer(d):
        return (z * NY + lax.rem(y + d, NY), t)

    def t_peer(d):
        return (dp, lax.rem(t + d, NT))

    following = (lax.rem(dp + 1, NZ * NY), t)
    preceding = (lax.rem(dp + NZ * NY - 1, NZ * NY), t)
    barrier = pltpu.get_barrier_semaphore()
    peers = [preceding] + [y_peer(d) for d in range(1, NY)] + [z_peer(d) for d in range(1, NZ)]
    peers += [t_peer(d) for d in range(1, NT)]
    for peer in peers:
        pl.semaphore_signal(barrier, inc=1, device_id=peer, device_id_type=MESH)

    def remote(src, dst, send, recv, peer):
        return pltpu.make_async_remote_copy(
            src_ref=src, dst_ref=dst, send_sem=send, recv_sem=recv, device_id=peer, device_id_type=MESH
        )

    def wait_for(ref, sem):
        pltpu.make_async_copy(ref, ref, sem).wait()

    earlier, later = pl.ds(0, TOK), pl.ds(TOK, TOK)
    loads = [(len_hbm, lengths), (k_hbm, keys.at[later]), (v_hbm, vals.at[later]), (q_hbm, q_ref)]
    loads = [pltpu.make_async_copy(src, dst, l_sem.at[n]) for n, (src, dst) in enumerate(loads)]
    for load in loads:
        load.start()

    pl.semaphore_wait(barrier, len(peers))
    halo = []
    for b in reversed(range(TOK // QB)):
        rows = pl.ds(b * QB, QB)
        halo += [
            remote(src.at[rows], dst.at[rows], h_send.at[i, b], h_recv.at[i, b], following)
            for i, (src, dst) in enumerate(((k_hbm, keys), (v_hbm, vals)))
        ]
    for copy in halo:
        copy.start()

    loads[0].wait()
    lens = lengths[...].astype(F32)
    n_docs = lens.shape[1]
    before = lax.broadcasted_iota(jnp.int32, (n_docs, n_docs), 1) < lax.broadcasted_iota(
        jnp.int32, (n_docs, n_docs), 0
    )
    starts = jnp.sum(jnp.where(before, lens, 0.0), axis=1, keepdims=True)
    position = (first_row + lax.broadcasted_iota(jnp.int32, (1, TOK), 1)).astype(F32)
    doc_start = jnp.max(jnp.where(starts <= position, starts, 0.0), axis=0, keepdims=True)
    for b in range(TOK // QB):
        key_pos = (first_row - TOK + b * QB + lax.broadcasted_iota(jnp.int32, (WIN, QB), 0)).astype(F32)
        cols = slice(b * QB, (b + 1) * QB)
        visible = (key_pos >= doc_start[:, cols]) & (key_pos <= position[:, cols])
        bias[b] = jnp.where(visible, 0.0, -1e30)
    for load in loads[1:]:
        load.wait()
    vt[:, TOK:] = vals[TOK:].T

    factor = math.log2(math.e) / math.sqrt(HD)

    def attend(pair, b, energy):
        rows = pl.ds(pl.multiple_of(b * QB, QB), QB)
        window = pl.ds(pl.multiple_of(b * QB, QB), WIN)
        two = jnp.concatenate(
            [q_ref[rows, h * HD : (h + 1) * HD] for h in (pair, pair + PAIRS)], axis=0
        )
        scores = lax.dot_general(
            keys[window, :], two, (((1,), (1,)), ((), ())), preferred_element_type=F32
        )
        mask = bias[b]
        scores = scores * factor + jnp.concatenate([mask, mask], axis=1)
        peak = jnp.max(scores, axis=0, keepdims=True)
        exponent = jnp.exp2(scores - peak)
        total = jnp.sum(exponent, axis=0, keepdims=True)
        blended = lax.dot_general(
            vt[:, window], exponent.astype(jnp.bfloat16), (((1,), (0,)), ((), ())), preferred_element_type=F32
        )
        attended = (blended * (1.0 / total)).astype(jnp.bfloat16)
        at[pair, 0:HD, rows] = attended[:, 0:QB]
        at[pair, HD:, rows] = attended[:, QB:]
        wide = attended.astype(F32)
        return energy + jnp.sum(wide * wide, axis=0, keepdims=True)

    def gram_block(k, row, col):
        block = lax.dot_general(at[row], at[col], (((1,), (1,)), ((), ())), preferred_element_type=F32)
        gs[...] = block
        fixed, scale = to_fixed(block)
        yqs[k] = scale
        for q in range(4):
            for a in range(NY):
                low = q * 64 + a * 16
                yq[a, k, q * 16 : (q + 1) * 16, :] = fixed[low : low + 16, :]
            own[k, q * 16 : (q + 1) * 16, :] = gs[pl.ds(pl.multiple_of(q * 64 + y * 16, 16), 16), :]

    def y_stage(piece):
        first, blocks = FIRST[piece], PIECES[piece][1]
        for i, (row, col) in enumerate(blocks):
            gram_block(first + i, row, col)
        span = pl.ds(first, len(blocks))
        for d in range(1, NY):
            peer = y_peer(d)
            to = lax.rem(y + d, NY)
            remote(yqs.at[span], yrs.at[d - 1, span], y_send.at[1, piece], y_recv.at[1, piece], peer).start()
            remote(yq.at[to, span], yr.at[d - 1, span], y_send.at[0, piece], y_recv.at[0, piece], peer).start()

    def z_stage(piece):
        first, blocks = FIRST[piece], PIECES[piece][1]
        span = pl.ds(first, len(blocks))
        wait_for(yrs.at[:, span], y_recv.at[1, piece])
        wait_for(yr.at[:, span], y_recv.at[0, piece])
        for k in range(first, first + len(blocks)):
            total = own[k]
            for d in range(NY - 1):
                total = total + from_fixed(yr[d, k], yrs[d, k])
            own[k] = total
            fixed, scale = to_fixed(total)
            zqs[k] = scale
            for q in range(4):
                zq[k, q] = fixed[q * 16 : (q + 1) * 16, :]
        for role, offsets in enumerate(INPUTS):
            for n, offset in enumerate(offsets):

                def forward(blocks, quarter, slots, role=role, n=n, offset=offset):
                    peer = z_peer(NZ - offset + RELAYS[role])
                    i = 3 * role + n
                    col = slots.start
                    remote(
                        zqs.at[blocks], rrs.at[role, n, slots], r_send.at[1, i], r_recv.at[1, role, col], peer
                    ).start()
                    remote(
                        zq.at[blocks, quarter], rr.at[role, n, slots], r_send.at[0, i], r_recv.at[0, role, col], peer
                    ).start()

                for_owner(piece, offset, forward)

    def for_owner(piece, offset, action):
        stage, blocks = PIECES[piece]
        owner = lax.rem(z + NZ - offset, NZ)
        pair = lax.div(lax.rem(owner, 8), 2)
        quarter = 2 * lax.div(owner, 8) + lax.rem(owner, 2)
        if blocks[0][0] == stage:

            @pl.when(pair == stage)
            def _():
                action(pl.ds(FIRST[piece], len(blocks)), quarter, pl.ds(blocks[0][1], len(blocks)))

        else:

            @pl.when(pair < stage)
            def _():
                action(pl.ds(FIRST[piece] + pair, 1), quarter, pl.ds(stage, 1))

    def z_relay(piece):
        for role, offset in enumerate(RELAYS):

            def pass_on(blocks, quarter, slots, role=role, offset=offset):
                inputs, col = len(INPUTS[role]), slots.start
                wait_for(rrs.at[role, pl.ds(0, inputs), slots], r_recv.at[1, role, col])
                wait_for(rr.at[role, pl.ds(0, inputs), slots], r_recv.at[0, role, col])
                rows = pl.ds(pl.multiple_of(quarter * 16, 16), 16)
                for i in range(slots.size):
                    total = own[blocks.start + i, rows, :]
                    for n in range(inputs):
                        total = total + from_fixed(rr[role, n, col + i], rrs[role, n, col + i])
                    rq[role, col + i], rqs[role, col + i] = to_fixed(total)
                peer = z_peer(NZ - offset)
                remote(rqs.at[role, slots], zrs.at[role, slots], z_send.at[1, role], z_recv.at[1, col], peer).start()
                remote(rq.at[role, slots], zr.at[role, slots], z_send.at[0, role], z_recv.at[0, col], peer).start()

            for_owner(piece, offset, pass_on)

    def of_stage(stage, step):
        for piece, (its_stage, _) in enumerate(PIECES):
            if its_stage == stage:
                step(piece)

    def spread(n, landing, peer):
        for d in range(1, landing.shape[0] + 1):
            remote(en.at[n], landing.at[d - 1], e_send.at[n], e_recv.at[n], peer(d)).start()

    def gather(n, landing):
        wait_for(landing, e_recv.at[n])
        return en[n] + jnp.sum(landing[...], axis=0)

    energy = jnp.zeros((1, 2 * QB), F32)
    for pair in range(PAIRS):
        if pair == 0:
            for n, b in enumerate(reversed(range(TOK // QB))):
                for copy in halo[2 * n : 2 * n + 2]:
                    copy.wait_recv()
                rows = slice(b * QB, (b + 1) * QB)
                vt[:, rows] = vals[rows].T
                energy = attend(pair, jnp.int32(b), energy)
        else:
            energy = lax.fori_loop(0, TOK // QB, functools.partial(attend, pair), energy, unroll=4)
        if pair == PAIRS - 1:
            en[0] = energy[:, 0:QB] + energy[:, QB:]
            spread(0, enz, z_peer)
        of_stage(pair, y_stage)
    last = [piece for piece, (stage, _) in enumerate(PIECES) if stage == PAIRS - 1]
    of_stage(0, z_stage)
    of_stage(1, z_stage)
    of_stage(0, z_relay)
    of_stage(PAIRS - 2, z_stage)
    of_stage(PAIRS - 3, z_relay)
    en[1] = gather(0, enz)
    spread(1, ent, t_peer)
    of_stage(PAIRS - 2, z_relay)
    z_stage(last[0])
    en[2] = gather(1, ent)
    spread(2, eny, y_peer)
    z_stage(last[1])
    z_relay(last[0])
    z_relay(last[1])

    my_pair = lax.div(lax.rem(z, 8), 2)
    my_quarter = 2 * lax.div(z, 8) + lax.rem(z, 2)
    all_energy = jnp.sum(gather(2, eny), axis=1, keepdims=True)
    gain = (HEADS * HD) / all_energy
    for piece in range(len(PIECES)):

        def arrive(blocks, quarter, slots):
            wait_for(zrs.at[:, slots], z_recv.at[1, slots.start])
            wait_for(zr.at[:, slots], z_recv.at[0, slots.start])

        for_owner(piece, 0, arrive)

    row_id = dp * 16 + lax.broadcasted_iota(jnp.int32, (16, HD), 0)
    col_id = lax.broadcasted_iota(jnp.int32, (16, HD), 1)
    my_rows = pl.ds(pl.multiple_of(my_quarter * 16, 16), 16)
    for col in range(PAIRS):
        k = sum(jnp.where(my_pair == row, NUMBER[row, col], 0) for row in range(PAIRS))
        total = own[k, my_rows, :]
        for role in range(len(RELAYS)):
            total = total + from_fixed(zr[role, col], zrs[role, col])
        for half in range(2):
            head = col + PAIRS * half
            part = total[:, half * HD : (half + 1) * HD] * gain
            eye = jnp.where(row_id == col_id + head * HD, damping, 0.0)
            out_ref[:, head * HD : (head + 1) * HD] = part + eye

    for copy in halo:
        copy.wait_send()
    for piece, (_, blocks) in enumerate(PIECES):
        span = pl.ds(FIRST[piece], len(blocks))
        wait_for(yrs.at[:, span], y_send.at[1, piece])
        wait_for(yr.at[:, span], y_send.at[0, piece])
    for role, offsets in enumerate(INPUTS):
        for n in range(len(offsets)):
            wait_for(rrs.at[role, n], r_send.at[1, 3 * role + n])
            wait_for(rr.at[role, n], r_send.at[0, 3 * role + n])
        wait_for(zrs.at[role], z_send.at[1, role])
        wait_for(zr.at[role], z_send.at[0, role])
    for n, landing in enumerate((enz, ent, eny)):
        wait_for(landing, e_send.at[n])


def on_device(queries, key_heads, value_heads, doc_lengths):
    blocks = PAIRS * PAIRS
    width = 2 * HD
    roles = len(RELAYS)
    vmem = pl.BlockSpec(memory_space=pltpu.VMEM)
    rows = pl.pallas_call(
        kernel,
        out_shape=jax.ShapeDtypeStruct((16, 8 * HD), F32),
        in_specs=[pl.BlockSpec(memory_space=pl.ANY)] * 4,
        out_specs=vmem,
        scratch_shapes=[
            pltpu.VMEM((1, doc_lengths.shape[0]), jnp.int32),
            pltpu.VMEM((TOK, 8 * HD), jnp.bfloat16),
            pltpu.VMEM((2 * TOK, HD), jnp.bfloat16),
            pltpu.VMEM((2 * TOK, HD), jnp.bfloat16),
            pltpu.VMEM((HD, 2 * TOK), jnp.bfloat16),
            pltpu.VMEM((TOK // QB, WIN, QB), F32),
            pltpu.VMEM((PAIRS, width, TOK), jnp.bfloat16),
            pltpu.VMEM((width, width), F32),
            pltpu.VMEM((blocks, 64, width), F32),
            pltpu.VMEM((NY, blocks, 64, width), jnp.int16),
            pltpu.VMEM((blocks, 1, width), F32),
            pltpu.VMEM((NY - 1, blocks, 64, width), jnp.int16),
            pltpu.VMEM((NY - 1, blocks, 1, width), F32),
            pltpu.VMEM((blocks, 4, 16, width), jnp.int16),
            pltpu.VMEM((blocks, 1, width), F32),
            pltpu.VMEM((roles, 3, PAIRS, 16, width), jnp.int16),
            pltpu.VMEM((roles, 3, PAIRS, 1, width), F32),
            pltpu.VMEM((roles, PAIRS, 16, width), jnp.int16),
            pltpu.VMEM((roles, PAIRS, 1, width), F32),
            pltpu.VMEM((roles, PAIRS, 16, width), jnp.int16),
            pltpu.VMEM((roles, PAIRS, 1, width), F32),
            pltpu.VMEM((3, 1, HD), F32),
            pltpu.VMEM((NT - 1, 1, HD), F32),
            pltpu.VMEM((NY - 1, 1, HD), F32),
            pltpu.VMEM((NZ - 1, 1, HD), F32),
            pltpu.SemaphoreType.DMA((4,)),
            pltpu.SemaphoreType.DMA((2, TOK // QB)),
            pltpu.SemaphoreType.DMA((2, TOK // QB)),
            pltpu.SemaphoreType.DMA((2, len(PIECES))),
            pltpu.SemaphoreType.DMA((2, len(PIECES))),
            pltpu.SemaphoreType.DMA((2, 3 * roles)),
            pltpu.SemaphoreType.DMA((2, roles, PAIRS)),
            pltpu.SemaphoreType.DMA((2, roles)),
            pltpu.SemaphoreType.DMA((2, PAIRS)),
            pltpu.SemaphoreType.DMA((3,)),
            pltpu.SemaphoreType.DMA((3,)),
        ],
        compiler_params=pltpu.CompilerParams(
            collective_id=0, has_side_effects=True, vmem_limit_bytes=60 << 20
        ),
        name="attend_and_gram",
    )(doc_lengths.reshape(1, -1), queries, key_heads, value_heads)
    return rows[None]


def solution(mesh):
    placed = (P("dp", "tensor"), P("dp", "tensor"), P("dp", "tensor"), P())
    return jax.shard_map(
        on_device, mesh=mesh, in_specs=placed, out_specs=P("tensor", "dp", None), check_vma=False
    )
```

```python
import functools
import math

import jax
import jax.numpy as jnp
from jax import lax
from jax.experimental import pallas as pl
from jax.experimental.pallas import tpu as pltpu
from jax.sharding import PartitionSpec as P

HEADS = 64
HD = 128
TOK = 512
QB = 128
WIN = TOK + QB
NZ, NY, NT = 16, 4, 8
PAIRS = 4
FULL = 32767.0
MESH = pl.DeviceIdType.MESH
F32 = jnp.float32

damping = 0.01


RELAYS = (1, 5, 15, 11)
INPUTS = ((2, 3, 4), (6, 7, 8), (14, 13, 12), (10, 9))


def plan():
    pieces = []
    for stage in range(PAIRS):
        row = [(stage, col) for col in range(stage + 1)]
        if stage == PAIRS - 1:
            pieces.append((stage, row))
        else:
            pieces.append((stage, row))
        if stage > 0:
            pieces.append((stage, [(above, stage) for above in range(stage)]))
    return pieces


PIECES = plan()
FIRST = [sum(len(blocks) for _, blocks in PIECES[:n]) for n in range(len(PIECES))]

def to_fixed(block):
    peak = jnp.maximum(jnp.max(jnp.abs(block), axis=0, keepdims=True), 1e-30)
    fixed = jnp.round(block * (FULL / peak)).astype(jnp.int32).astype(jnp.int16)
    return fixed, peak * (1.0 / FULL)


def from_fixed(fixed, scale):
    return fixed.astype(jnp.int32).astype(F32) * scale


def kernel(
    len_hbm, q_hbm, k_hbm, v_hbm, out_ref,
    lengths, q_ref, keys, vals, vt, bias, at, gs, own,
    yq, yqs, yr, yrs, zq, zqs, rr, rrs, rq, rqs, zr, zrs, en, ent, eny, enz,
    l_sem, h_send, h_recv, y_send, y_recv, r_send, r_recv, z_send, z_recv, e_send, e_recv,
):
    dp = lax.axis_index("dp")
    t = lax.axis_index("tensor")
    z, y = lax.div(dp, NY), lax.rem(dp, NY)
    first_row = dp * TOK

    def z_peer(d):
        return (lax.rem(z + d, NZ) * NY + y, t)

    def y_peer(d):
        return (z * NY + lax.rem(y + d, NY), t)

    def t_peer(d):
        return (dp, lax.rem(t + d, NT))

    following = (lax.rem(dp + 1, NZ * NY), t)
    preceding = (lax.rem(dp + NZ * NY - 1, NZ * NY), t)
    barrier = pltpu.get_barrier_semaphore()
    peers = [preceding] + [y_peer(d) for d in range(1, NY)] + [z_peer(d) for d in range(1, NZ)]
    peers += [t_peer(d) for d in range(1, NT)]
    for peer in peers:
        pl.semaphore_signal(barrier, inc=1, device_id=peer, device_id_type=MESH)

    def remote(src, dst, send, recv, peer):
        return pltpu.make_async_remote_copy(
            src_ref=src, dst_ref=dst, send_sem=send, recv_sem=recv, device_id=peer, device_id_type=MESH
        )

    def wait_for(ref, sem):
        pltpu.make_async_copy(ref, ref, sem).wait()

    earlier, later = pl.ds(0, TOK), pl.ds(TOK, TOK)
    loads = [(len_hbm, lengths), (k_hbm, keys.at[later]), (v_hbm, vals.at[later]), (q_hbm, q_ref)]
    loads = [pltpu.make_async_copy(src, dst, l_sem.at[n]) for n, (src, dst) in enumerate(loads)]
    for load in loads:
        load.start()

    pl.semaphore_wait(barrier, len(peers))
    halo = []
    for b in reversed(range(TOK // QB)):
        rows = pl.ds(b * QB, QB)
        halo += [
            remote(src.at[rows], dst.at[rows], h_send.at[i, b], h_recv.at[i, b], following)
            for i, (src, dst) in enumerate(((k_hbm, keys), (v_hbm, vals)))
        ]
    for copy in halo:
        copy.start()

    loads[0].wait()
    lens = lengths[...].astype(F32)
    n_docs = lens.shape[1]
    before = lax.broadcasted_iota(jnp.int32, (n_docs, n_docs), 1) < lax.broadcasted_iota(
        jnp.int32, (n_docs, n_docs), 0
    )
    starts = jnp.sum(jnp.where(before, lens, 0.0), axis=1, keepdims=True)
    position = (first_row + lax.broadcasted_iota(jnp.int32, (1, TOK), 1)).astype(F32)
    doc_start = jnp.max(jnp.where(starts <= position, starts, 0.0), axis=0, keepdims=True)
    for b in range(TOK // QB):
        key_pos = (first_row - TOK + b * QB + lax.broadcasted_iota(jnp.int32, (WIN, QB), 0)).astype(F32)
        cols = slice(b * QB, (b + 1) * QB)
        visible = (key_pos >= doc_start[:, cols]) & (key_pos <= position[:, cols])
        bias[b] = jnp.where(visible, 0.0, -1e30)
    for load in loads[1:]:
        load.wait()
    vt[:, TOK:] = vals[TOK:].T

    factor = math.log2(math.e) / math.sqrt(HD)

    def attend(pair, b, energy):
        rows = pl.ds(pl.multiple_of(b * QB, QB), QB)
        window = pl.ds(pl.multiple_of(b * QB, QB), WIN)
        two = jnp.concatenate(
            [q_ref[rows, h * HD : (h + 1) * HD] for h in (pair, pair + PAIRS)], axis=0
        )
        scores = lax.dot_general(
            keys[window, :], two, (((1,), (1,)), ((), ())), preferred_element_type=F32
        )
        mask = bias[b]
        scores = scores * factor + jnp.concatenate([mask, mask], axis=1)
        peak = jnp.max(scores, axis=0, keepdims=True)
        exponent = jnp.exp2(scores - peak)
        total = jnp.sum(exponent, axis=0, keepdims=True)
        blended = lax.dot_general(
            vt[:, window], exponent.astype(jnp.bfloat16), (((1,), (0,)), ((), ())), preferred_element_type=F32
        )
        attended = (blended * (1.0 / total)).astype(jnp.bfloat16)
        at[pair, 0:HD, rows] = attended[:, 0:QB]
        at[pair, HD:, rows] = attended[:, QB:]
        wide = attended.astype(F32)
        return energy + jnp.sum(wide * wide, axis=0, keepdims=True)

    def gram_block(k, row, col):
        block = lax.dot_general(at[row], at[col], (((1,), (1,)), ((), ())), preferred_element_type=F32)
        gs[...] = block
        fixed, scale = to_fixed(block)
        yqs[k] = scale
        for q in range(4):
            for a in range(NY):
                low = q * 64 + a * 16
                yq[a, k, q * 16 : (q + 1) * 16, :] = fixed[low : low + 16, :]
            own[PAIRS * row + col, q * 16 : (q + 1) * 16, :] = gs[pl.ds(pl.multiple_of(q * 64 + y * 16, 16), 16), :]

    def y_stage(piece):
        first, blocks = FIRST[piece], PIECES[piece][1]
        for i, (row, col) in enumerate(blocks):
            gram_block(first + i, row, col)
        span = pl.ds(first, len(blocks))
        for d in range(1, NY):
            peer = y_peer(d)
            to = lax.rem(y + d, NY)
            remote(yqs.at[span], yrs.at[d - 1, span], y_send.at[1, piece], y_recv.at[1, piece], peer).start()
            remote(yq.at[to, span], yr.at[d - 1, span], y_send.at[0, piece], y_recv.at[0, piece], peer).start()

    def z_stage(part):
        for piece, (stage, blocks) in enumerate(PIECES):
            if part != (0 if stage < PAIRS - 1 else 1 if blocks[0][0] == stage else 2):
                continue
            span = pl.ds(FIRST[piece], len(blocks))
            wait_for(yrs.at[:, span], y_recv.at[1, piece])
            wait_for(yr.at[:, span], y_recv.at[0, piece])
            for i, (row, col) in enumerate(blocks):
                k, place = FIRST[piece] + i, PAIRS * row + col
                total = own[place]
                for d in range(NY - 1):
                    total = total + from_fixed(yr[d, k], yrs[d, k])
                own[place] = total
                fixed, scale = to_fixed(total)
                zqs[place] = scale
                for q in range(4):
                    zq[place, q] = fixed[q * 16 : (q + 1) * 16, :]
        for role, offsets in enumerate(INPUTS):
            for n, offset in enumerate(offsets):

                def forward(blocks, quarter, slots, role=role, n=n, offset=offset):
                    peer = z_peer(NZ - offset + RELAYS[role])
                    i = 3 * role + n
                    col = slots.start
                    remote(
                        zqs.at[blocks], rrs.at[role, n, slots], r_send.at[1, i], r_recv.at[1, role, col], peer
                    ).start()
                    remote(
                        zq.at[blocks, quarter], rr.at[role, n, slots], r_send.at[0, i], r_recv.at[0, role, col], peer
                    ).start()

                for_owner(part, offset, forward)

    def for_owner(part, offset, action):
        owner = lax.rem(z + NZ - offset, NZ)
        pair = lax.div(lax.rem(owner, 8), 2)
        quarter = 2 * lax.div(owner, 8) + lax.rem(owner, 2)
        low, count = ((0, PAIRS - 1), (0, PAIRS), (PAIRS - 1, 1))[part]

        @pl.when(pair == PAIRS - 1 if part == 1 else pair < PAIRS - 1)
        def _():
            action(pl.ds(PAIRS * pair + low, count), quarter, pl.ds(low, count))

    def z_relay(part):
        for role, offset in enumerate(RELAYS):

            def pass_on(blocks, quarter, slots, role=role, offset=offset):
                inputs, col = len(INPUTS[role]), slots.start
                wait_for(rrs.at[role, pl.ds(0, inputs), slots], r_recv.at[1, role, col])
                wait_for(rr.at[role, pl.ds(0, inputs), slots], r_recv.at[0, role, col])
                rows = pl.ds(pl.multiple_of(quarter * 16, 16), 16)
                for i in range(slots.size):
                    total = own[blocks.start + i, rows, :]
                    for n in range(inputs):
                        total = total + from_fixed(rr[role, n, col + i], rrs[role, n, col + i])
                    rq[role, col + i], rqs[role, col + i] = to_fixed(total)
                peer = z_peer(NZ - offset)
                remote(rqs.at[role, slots], zrs.at[role, slots], z_send.at[1, role], z_recv.at[1, col], peer).start()
                remote(rq.at[role, slots], zr.at[role, slots], z_send.at[0, role], z_recv.at[0, col], peer).start()

            for_owner(part, offset, pass_on)

    def of_stage(stage, step):
        for piece, (its_stage, _) in enumerate(PIECES):
            if its_stage == stage:
                step(piece)

    def spread(n, landing, peer):
        for d in range(1, landing.shape[0] + 1):
            remote(en.at[n], landing.at[d - 1], e_send.at[n], e_recv.at[n], peer(d)).start()

    def gather(n, landing):
        wait_for(landing, e_recv.at[n])
        return en[n] + jnp.sum(landing[...], axis=0)

    energy = jnp.zeros((1, 2 * QB), F32)
    for pair in range(PAIRS):
        if pair == 0:
            for n, b in enumerate(reversed(range(TOK // QB))):
                for copy in halo[2 * n : 2 * n + 2]:
                    copy.wait_recv()
                rows = slice(b * QB, (b + 1) * QB)
                vt[:, rows] = vals[rows].T
                energy = attend(pair, jnp.int32(b), energy)
        else:
            energy = lax.fori_loop(0, TOK // QB, functools.partial(attend, pair), energy, unroll=4)
        if pair == PAIRS - 1:
            en[0] = energy[:, 0:QB] + energy[:, QB:]
            spread(0, enz, z_peer)
        of_stage(pair, y_stage)
    last = [piece for piece, (stage, _) in enumerate(PIECES) if stage == PAIRS - 1]
    z_stage(0)
    en[1] = gather(0, enz)
    spread(1, ent, t_peer)
    z_relay(0)
    z_stage(1)
    en[2] = gather(1, ent)
    spread(2, eny, y_peer)
    z_stage(2)
    z_relay(1)
    z_relay(2)

    my_pair = lax.div(lax.rem(z, 8), 2)
    my_quarter = 2 * lax.div(z, 8) + lax.rem(z, 2)
    all_energy = jnp.sum(gather(2, eny), axis=1, keepdims=True)
    gain = (HEADS * HD) / all_energy
    for part in range(3):

        def arrive(blocks, quarter, slots):
            wait_for(zrs.at[:, slots], z_recv.at[1, slots.start])
            wait_for(zr.at[:, slots], z_recv.at[0, slots.start])

        for_owner(part, 0, arrive)

    row_id = dp * 16 + lax.broadcasted_iota(jnp.int32, (16, HD), 0)
    col_id = lax.broadcasted_iota(jnp.int32, (16, HD), 1)
    my_rows = pl.ds(pl.multiple_of(my_quarter * 16, 16), 16)
    for col in range(PAIRS):
        total = own[PAIRS * my_pair + col, my_rows, :]
        for role in range(len(RELAYS)):
            total = total + from_fixed(zr[role, col], zrs[role, col])
        for half in range(2):
            head = col + PAIRS * half
            part = total[:, half * HD : (half + 1) * HD] * gain
            eye = jnp.where(row_id == col_id + head * HD, damping, 0.0)
            out_ref[:, head * HD : (head + 1) * HD] = part + eye

    for copy in halo:
        copy.wait_send()
    for piece, (_, blocks) in enumerate(PIECES):
        span = pl.ds(FIRST[piece], len(blocks))
        wait_for(yrs.at[:, span], y_send.at[1, piece])
        wait_for(yr.at[:, span], y_send.at[0, piece])
    for role, offsets in enumerate(INPUTS):
        for n in range(len(offsets)):
            wait_for(rrs.at[role, n], r_send.at[1, 3 * role + n])
            wait_for(rr.at[role, n], r_send.at[0, 3 * role + n])
        wait_for(zrs.at[role], z_send.at[1, role])
        wait_for(zr.at[role], z_send.at[0, role])
    for n, landing in enumerate((enz, ent, eny)):
        wait_for(landing, e_send.at[n])


def on_device(queries, key_heads, value_heads, doc_lengths):
    blocks = PAIRS * PAIRS
    width = 2 * HD
    roles = len(RELAYS)
    vmem = pl.BlockSpec(memory_space=pltpu.VMEM)
    rows = pl.pallas_call(
        kernel,
        out_shape=jax.ShapeDtypeStruct((16, 8 * HD), F32),
        in_specs=[pl.BlockSpec(memory_space=pl.ANY)] * 4,
        out_specs=vmem,
        scratch_shapes=[
            pltpu.VMEM((1, doc_lengths.shape[0]), jnp.int32),
            pltpu.VMEM((TOK, 8 * HD), jnp.bfloat16),
            pltpu.VMEM((2 * TOK, HD), jnp.bfloat16),
            pltpu.VMEM((2 * TOK, HD), jnp.bfloat16),
            pltpu.VMEM((HD, 2 * TOK), jnp.bfloat16),
            pltpu.VMEM((TOK // QB, WIN, QB), F32),
            pltpu.VMEM((PAIRS, width, TOK), jnp.bfloat16),
            pltpu.VMEM((width, width), F32),
            pltpu.VMEM((blocks, 64, width), F32),
            pltpu.VMEM((NY, blocks, 64, width), jnp.int16),
            pltpu.VMEM((blocks, 1, width), F32),
            pltpu.VMEM((NY - 1, blocks, 64, width), jnp.int16),
            pltpu.VMEM((NY - 1, blocks, 1, width), F32),
            pltpu.VMEM((blocks, 4, 16, width), jnp.int16),
            pltpu.VMEM((blocks, 1, width), F32),
            pltpu.VMEM((roles, 3, PAIRS, 16, width), jnp.int16),
            pltpu.VMEM((roles, 3, PAIRS, 1, width), F32),
            pltpu.VMEM((roles, PAIRS, 16, width), jnp.int16),
            pltpu.VMEM((roles, PAIRS, 1, width), F32),
            pltpu.VMEM((roles, PAIRS, 16, width), jnp.int16),
            pltpu.VMEM((roles, PAIRS, 1, width), F32),
            pltpu.VMEM((3, 1, HD), F32),
            pltpu.VMEM((NT - 1, 1, HD), F32),
            pltpu.VMEM((NY - 1, 1, HD), F32),
            pltpu.VMEM((NZ - 1, 1, HD), F32),
            pltpu.SemaphoreType.DMA((4,)),
            pltpu.SemaphoreType.DMA((2, TOK // QB)),
            pltpu.SemaphoreType.DMA((2, TOK // QB)),
            pltpu.SemaphoreType.DMA((2, len(PIECES))),
            pltpu.SemaphoreType.DMA((2, len(PIECES))),
            pltpu.SemaphoreType.DMA((2, 3 * roles)),
            pltpu.SemaphoreType.DMA((2, roles, PAIRS)),
            pltpu.SemaphoreType.DMA((2, roles)),
            pltpu.SemaphoreType.DMA((2, PAIRS)),
            pltpu.SemaphoreType.DMA((3,)),
            pltpu.SemaphoreType.DMA((3,)),
        ],
        compiler_params=pltpu.CompilerParams(
            collective_id=0, has_side_effects=True, vmem_limit_bytes=60 << 20
        ),
        name="attend_and_gram",
    )(doc_lengths.reshape(1, -1), queries, key_heads, value_heads)
    return rows[None]


def solution(mesh):
    placed = (P("dp", "tensor"), P("dp", "tensor"), P("dp", "tensor"), P())
    return jax.shard_map(
        on_device, mesh=mesh, in_specs=placed, out_specs=P("tensor", "dp", None), check_vma=False
    )
```
